32 devices in a mesh: dp: 4 (over y, core), tensor: 8 (over z, x).
Axes of the slice: x: 2, y: 2, z: 4, core: 2. Of those that a mesh axis runs over, the one named last changes fastest.
Arguments:
- features: bfloat16 [512, 4096], P('dp'), may hold values from -6 to 6
- enc_in: bfloat16 [4096, 2048], P(None, 'tensor'), may hold values from -0.09375 to 0.09375
- enc_out: bfloat16 [2048, 8192], P('tensor'), may hold values from -0.125 to 0.125
- noise: bfloat16 [512, 4096], P('dp', 'tensor'), may hold values from -6 to 6
- in_weight: bfloat16 [4096, 16384], P('dp', 'tensor'), may hold values from -0.09375 to 0.09375
- out_weight: bfloat16 [4096, 16384], P('dp', 'tensor'), may hold values from -0.046875 to 0.046875
- probes: bfloat16 [2, 512, 4096], P(None, 'dp'), may hold values from -6 to 6
Outputs:
- flowed: float32 [512, 4096], P('dp', 'tensor')
- logdet: float32 [512], P('dp')
The draws below stay inside these ranges and needn't reach their ends.
All inputs are finite; a program needn't handle non-finite values.
Results may differ from the reference program's by a relative error of at most 0.017.
Values may be sent and summed in bfloat16 or wider, within the bound.
A program may use at most 128 MiB of HBM per device.

```python
import jax
import jax.numpy as jnp

L = 4096
H = 16384
DX = 4096
HE = 2048
PROBES = 2
TERMS = 3
ROWS = 512


def shard_levels(stream_key, shape, pieces, low, high):
    level, own = 1.0, jax.random.fold_in(stream_key, 6)
    for position, shards_of in pieces:
        draws = jnp.exp(jax.random.uniform(jax.random.fold_in(own, position), (shards_of,), jnp.float32, low / len(pieces), high / len(pieces)))
        level = level * jnp.repeat(draws, shape[position] // shards_of).reshape([-1 if axis == position else 1 for axis in range(len(shape))])
    return level


def centred(stream_key, extent, deviation, limit, shards=(), held_as=jnp.bfloat16):
    loudness = shard_levels(stream_key, extent, shards, -0.22, 0.18) if shards else 1.0
    drawn = jax.random.normal(stream_key, extent, jnp.float32) * deviation * loudness
    return jnp.minimum(jnp.maximum(drawn, -limit), limit).astype(held_as)


def setup_inputs(seed: int = 0) -> dict:
    key_of = jax.random.split(jax.random.key(seed), 8)
    return {
        "features": centred(key_of[0], (ROWS, DX), 1.0, 6.0, ((0, 4),)),
        "enc_in": centred(key_of[1], (DX, HE), DX ** -0.5, 0.09375, ((1, 8),)),
        "enc_out": centred(key_of[2], (HE, 2 * L), HE ** -0.5, 0.125, ((0, 8),)),
        "noise": centred(key_of[3], (ROWS, L), 1.0, 6.0, ((0, 4), (1, 8))),
        "in_weight": centred(key_of[4], (L, H), L ** -0.5, 0.09375, ((0, 4), (1, 8))),
        "out_weight": centred(key_of[5], (L, H), H ** -0.5, 0.046875, ((0, 4), (1, 8))),
        "probes": centred(key_of[6], (PROBES, ROWS, L), 1.0, 6.0, ((1, 4),)),
    }


def reference(features, enc_in, enc_out, noise, in_weight, out_weight, probes):
    hidden = jax.nn.silu(jnp.dot(features, enc_in, preferred_element_type=jnp.float32)).astype(jnp.bfloat16)
    moments = jnp.dot(hidden, enc_out, preferred_element_type=jnp.float32)
    latent = (moments[:, :L] + jax.nn.softplus(moments[:, L:]) * noise.astype(jnp.float32)).astype(jnp.bfloat16)
    pre_act = jnp.dot(latent, in_weight, preferred_element_type=jnp.float32)
    tanh_val = jnp.tanh(pre_act)
    squash = tanh_val.astype(jnp.bfloat16)
    slope = 1.0 - tanh_val * tanh_val
    w_in32 = in_weight.astype(jnp.float32)
    w_out32 = out_weight.astype(jnp.float32)
    branch_sum = jnp.einsum("bh,lh->bl", squash.astype(jnp.float32), w_out32)
    flowed = latent.astype(jnp.float32) + branch_sum
    start32 = probes.astype(jnp.float32)
    current = probes
    running = jnp.zeros((probes.shape[1],), jnp.float32)
    for term_idx in range(TERMS):
        pulled = jnp.einsum("pbl,lh->pbh", current.astype(jnp.float32), w_out32)
        scaled = (pulled * slope[None]).astype(jnp.bfloat16)
        current = jnp.einsum("pbh,lh->pbl", scaled.astype(jnp.float32), w_in32).astype(jnp.bfloat16)
        coeff = (-1.0) ** term_idx / (term_idx + 1)
        running = running + coeff * jnp.sum(start32 * current.astype(jnp.float32), axis=(0, 2))
    logdet = running / PROBES
    return flowed, logdet
```

```python
import jax
import jax.numpy as jnp
from jax import lax
from jax.sharding import PartitionSpec as P


def dot(a, b):
    return jnp.dot(a, b, preferred_element_type=jnp.float32)


def dot_t(a, b):
    return lax.dot_general(a, b, (((1,), (1,)), ((), ())), preferred_element_type=jnp.float32)


def gather_blocks(shard, n):
    half = n // 2
    swap = [(d, d ^ 1) for d in range(n)]
    blocks = []
    for k in range(half):
        own = shard
        if k:
            own = lax.ppermute(
                shard, "dp", [(((y + k) % half) * 2 + c, y * 2 + c) for y in range(half) for c in range(2)]
            )
        blocks += [own, lax.ppermute(own, "dp", swap)]
    return blocks


def owners(n):
    me = lax.axis_index("dp")
    core = lax.rem(me, 2)
    y = lax.div(me, 2)
    half = n // 2
    out = []
    for k in range(half):
        yk = lax.rem(y + k, half)
        out += [yk * 2 + core, yk * 2 + 1 - core]
    return out


def make_local(n, t):
    def local(features, enc_in, enc_out, noise, in_weight, out_weight, probes):
        rows = features.shape[0]
        depth = in_weight.shape[0]
        latents = depth * n
        n_probes = probes.shape[0]
        w_in = gather_blocks(in_weight, n)
        w_out = gather_blocks(out_weight, n)
        own = owners(n)

        def cols(x):
            return [lax.dynamic_slice_in_dim(x, o * depth, depth, 1) for o in own]

        hidden = jax.nn.silu(dot(features, enc_in)).astype(jnp.bfloat16)
        partial_stats = dot(hidden, enc_out)
        moments = lax.psum_scatter(
            partial_stats.reshape(rows, 2, latents), "tensor", scatter_dimension=2, tiled=True
        )
        u_slice = (
            moments[:, 0] + jax.nn.softplus(moments[:, 1]) * noise.astype(jnp.float32)
        ).astype(jnp.bfloat16)
        u_full = lax.all_gather(u_slice, "tensor", axis=1, tiled=True)

        start = cols(probes.reshape(n_probes * rows, latents))
        q = sum(dot(a, w) for a, w in zip(start, w_in))
        pre_act = sum(dot(a, w) for a, w in zip(cols(u_full), w_in))
        tanh_val = jnp.tanh(pre_act)
        squash = tanh_val.astype(jnp.bfloat16)
        slope = jnp.tile(1.0 - tanh_val * tanh_val, (n_probes, 1))
        sq = q * slope
        sq16 = sq.astype(jnp.bfloat16)
        r = sum(dot(a, w) for a, w in zip(start, w_out))
        sr16 = (r * slope).astype(jnp.bfloat16)
        first = jnp.sum(sq * r, axis=1)

        both = [
            jnp.concatenate([dot_t(sr16, wi), dot_t(sq16, wo)], 0).astype(jnp.bfloat16)
            for wi, wo in zip(w_in, w_out)
        ]
        both = lax.psum(jnp.concatenate(both, 1), "tensor")
        w1, y1 = both[: n_probes * rows], both[n_probes * rows :]
        second = jnp.sum(w1.astype(jnp.float32) * y1.astype(jnp.float32), axis=1) / t
        left = sum(dot(y1[:, i * depth : (i + 1) * depth], w) for i, w in enumerate(w_in))
        right = sum(dot(w1[:, i * depth : (i + 1) * depth], w) for i, w in enumerate(w_out))
        third = jnp.sum(left * slope * right, axis=1)
        logdet = lax.psum(
            jnp.sum((first - second / 2 + third / 3).reshape(n_probes, rows), 0), "tensor"
        ) / n_probes

        branch = jnp.zeros((rows, latents), jnp.bfloat16)
        for o, w in zip(own, w_out):
            branch = lax.dynamic_update_slice_in_dim(
                branch, dot_t(squash, w).astype(jnp.bfloat16), o * depth, 1
            )
        flowed = u_slice.astype(jnp.float32) + lax.psum_scatter(
            branch, "tensor", scatter_dimension=1, tiled=True
        ).astype(jnp.float32)
        return flowed, logdet

    return local


def solution(mesh):
    in_specs = (
        P("dp", None),
        P(None, "tensor"),
        P("tensor", None),
        P("dp", "tensor"),
        P("dp", "tensor"),
        P("dp", "tensor"),
        P(None, "dp", None),
    )
    out_specs = (P("dp", "tensor"), P("dp"))
    local = make_local(mesh.shape["dp"], mesh.shape["tensor"])
    return jax.shard_map(local, mesh=mesh, in_specs=in_specs, out_specs=out_specs, check_vma=False)
```

```python
import functools

import jax
import jax.numpy as jnp
from jax import lax
from jax.experimental import pallas as pl
from jax.experimental.pallas import tpu as pltpu
from jax.sharding import PartitionSpec as P


def dot(a, b):
    return jnp.dot(a, b, preferred_element_type=jnp.float32)


def dot_t(a, b):
    return lax.dot_general(a, b, (((1,), (1,)), ((), ())), preferred_element_type=jnp.float32)


def gather_blocks(shard, n):
    half = n // 2
    swap = [(d, d ^ 1) for d in range(n)]
    blocks = []
    for k in range(half):
        own = shard
        if k:
            own = lax.ppermute(
                shard, "dp", [(((y + k) % half) * 2 + c, y * 2 + c) for y in range(half) for c in range(2)]
            )
        blocks += [own, lax.ppermute(own, "dp", swap)]
    return blocks


def owners(n):
    me = lax.axis_index("dp")
    core = lax.rem(me, 2)
    y = lax.div(me, 2)
    half = n // 2
    out = []
    for k in range(half):
        yk = lax.rem(y + k, half)
        out += [yk * 2 + core, yk * 2 + 1 - core]
    return out


def series_kernel(n, nt, nx, n_probes, *refs):
    w_in, w_out = refs[:n], refs[n : 2 * n]
    start, mix, slope, u_ref, flowed_ref, log_ref = refs[2 * n : 2 * n + 6]
    (win, wout, sr, full, sendx, xbuf, own, zbuf, left, right, pbuf, pxbuf, pzbuf,
     in_sem, out_sem, xs, xr, zs, zr, gs, gr, hs, hr, pxs, pxr, pzs, pzr) = refs[2 * n + 6 :]
    nz = nt // nx
    depth, hidden = w_in[0].shape
    big = start.shape[0]
    rows = big // n_probes
    chunk = win.shape[0] // nt
    tile = min(512, hidden)
    tiles = hidden // tile
    t = lax.axis_index("tensor")
    z, x = lax.div(t, nx), lax.rem(t, nx)

    def dev(zz, xx):
        return {"tensor": zz * nx + xx}

    def zup(k):
        return lax.rem(z + k, nz)

    def xup(j):
        return lax.rem(x + j, nx)

    def remote(src, dst, ss, rs, to):
        return pltpu.make_async_remote_copy(
            src_ref=src, dst_ref=dst, send_sem=ss, recv_sem=rs,
            device_id=to, device_id_type=pl.DeviceIdType.MESH,
        )

    barrier = pltpu.get_barrier_semaphore()
    for j in range(1, nx):
        pl.semaphore_signal(barrier, inc=1, device_id=dev(z, xup(j)), device_id_type=pl.DeviceIdType.MESH)
    for k in range(1, nz):
        pl.semaphore_signal(barrier, inc=1, device_id=dev(zup(k), x), device_id_type=pl.DeviceIdType.MESH)

    own_rows = [pl.ds(pl.multiple_of(o * depth, depth), depth) for o in owners(n)]
    loads_out = [pltpu.make_async_copy(w_out[b], wout.at[own_rows[b]], out_sem.at[b]) for b in range(n)]
    loads_in = [pltpu.make_async_copy(w_in[b], win.at[own_rows[b]], in_sem.at[b]) for b in range(n)]
    for c in loads_out + loads_in:
        c.start()

    def at(i):
        return pl.ds(pl.multiple_of(i * tile, tile), tile)

    for b in range(n):
        loads_out[b].wait()

        def pull(i, _):
            value = dot(start[:, own_rows[b]], wout[own_rows[b], at(i)])
            right[:, at(i)] = value if b == 0 else right[:, at(i)] + value
            return 0

        lax.fori_loop(0, tiles, pull, 0)
    totals = []
    for p in range(n_probes):
        band = pl.ds(p * rows, rows)

        def scale(i, acc):
            r = right[band, at(i)]
            sr[band, at(i)] = (r * slope[:, at(i)]).astype(jnp.bfloat16)
            return acc + jnp.sum(mix[band, at(i)].astype(jnp.float32) * r, axis=1, keepdims=True)

        totals.append(lax.fori_loop(0, tiles, scale, jnp.zeros((rows, 1), jnp.float32)))
    left[...] = jnp.zeros_like(left)
    right[...] = jnp.zeros_like(right)
    for c in loads_in:
        c.wait()
    pl.semaphore_wait(barrier, nx - 1 + nz - 1)

    def xcopy(s, j):
        return remote(sendx.at[s, j - 1], xbuf.at[s, j - 1], xs.at[s, j - 1], xr.at[s, j - 1], dev(z, xup(j)))

    def zcopy(s):
        return remote(own.at[s], zbuf.at[s], zs.at[s], zr.at[s], dev(zup(1 + s), x))

    def finish(s):
        for j in range(1, nx):
            xcopy(s, j).wait_recv()
        for i in range(own.shape[1] // rows):
            band = pl.ds(i * rows, rows)
            value = own[s, band, :].astype(jnp.float32)
            for j in range(1, nx):
                value += xbuf[s, j - 1, band, :].astype(jnp.float32)
            own[s, band, :] = value.astype(jnp.bfloat16)

    def scatter(s, _):
        for j in list(range(1, nx)) + [0]:
            off = pl.ds(pl.multiple_of((zup(1 + s) * nx + xup(j)) * chunk, chunk), chunk)
            dst = sendx.at[s, j - 1] if j else own.at[s]
            dst[pl.ds(0, big), :] = dot_t(sr[...], win[off, :]).astype(jnp.bfloat16)
            dst[pl.ds(big, big + rows), :] = dot_t(mix[...], wout[off, :]).astype(jnp.bfloat16)
            if j:
                xcopy(s, j).start()

        @pl.when(s >= 1)
        def _():
            finish(s - 1)
            zcopy(s - 1).start()

        return 0

    lax.fori_loop(0, nz, scatter, 0)
    finish(nz - 1)
    for s in range(nz - 1):
        zcopy(s).wait_recv()
    summed = []
    for i in range(own.shape[1] // rows):
        band = pl.ds(i * rows, rows)
        value = own[nz - 1, band, :].astype(jnp.float32)
        for s in range(nz - 1):
            value += zbuf[s, band, :].astype(jnp.float32)
        if i < 2 * n_probes:
            full[t, band, :] = value.astype(jnp.bfloat16)
        else:
            flowed_ref[...] = u_ref[...].astype(jnp.float32) + value

    def gcopy(k):
        return remote(full.at[t], full.at[t], gs.at[k - 1], gr.at[k - 1], dev(zup(k), x))

    def slot(k, j):
        return lax.rem(z + nz - k, nz) * nx + lax.rem(x + nx - j, nx)

    def hcopy(k, j):
        part = full.at[slot(k, 0)]
        return remote(part, part, hs.at[k, j - 1], hr.at[k, j - 1], dev(z, xup(j)))

    def harrive(k, j):
        part = full.at[slot(k, j)]
        return remote(part, part, hs.at[k, j - 1], hr.at[k, j - 1], dev(z, xup(j)))

    def garrive(k):
        part = full.at[slot(k, 0)]
        return remote(part, part, gs.at[k - 1], gr.at[k - 1], dev(zup(k), x))

    def consume(c):
        off = pl.ds(pl.multiple_of(c * chunk, chunk), chunk)

        def body(i, _):
            left[:, at(i)] += dot(full[c, pl.ds(big, big), :], win[off, at(i)])
            right[:, at(i)] += dot(full[c, pl.ds(0, big), :], wout[off, at(i)])
            return 0

        lax.fori_loop(0, tiles, body, 0)

    for k in range(1, nz):
        gcopy(k).start()
    for j in range(1, nx):
        hcopy(0, j).start()
    for p in range(n_probes):
        w1 = full[t, pl.ds(p * rows, rows), :].astype(jnp.float32)
        y1 = full[t, pl.ds(big + p * rows, rows), :].astype(jnp.float32)
        totals[p] -= 0.5 * jnp.sum(w1 * y1, axis=1, keepdims=True)
    consume(t)

    def gather(k, _):
        garrive(k).wait_recv()
        for j in range(1, nx):
            hcopy(k, j).start()
        consume(slot(k, 0))
        for j in range(1, nx):
            harrive(k - 1, j).wait_recv()
            consume(slot(k - 1, j))
        return 0

    lax.fori_loop(1, nz, gather, 0)
    for j in range(1, nx):
        harrive(nz - 1, j).wait_recv()
        consume(slot(nz - 1, j))

    total = jnp.zeros((rows, 1), jnp.float32)
    for p in range(n_probes):
        band = pl.ds(p * rows, rows)

        def last(i, acc):
            return acc + jnp.sum(left[band, at(i)] * slope[:, at(i)] * right[band, at(i)], axis=1, keepdims=True)

        third = lax.fori_loop(0, tiles, last, jnp.zeros((rows, 1), jnp.float32))
        total += totals[p] + third / 3.0

    def pxcopy(j):
        return remote(pbuf.at[0], pxbuf.at[j - 1], pxs.at[j - 1], pxr.at[j - 1], dev(z, xup(j)))

    def pzcopy(k):
        return remote(pbuf.at[1], pzbuf.at[k - 1], pzs.at[k - 1], pzr.at[k - 1], dev(zup(k), x))

    wide = jnp.broadcast_to(total / n_probes, (rows, 128))
    pbuf[0] = wide
    for j in range(1, nx):
        pxcopy(j).start()
    for j in range(1, nx):
        pxcopy(j).wait_recv()
        wide = wide + pxbuf[j - 1]
    pbuf[1] = wide
    for k in range(1, nz):
        pzcopy(k).start()
    for k in range(1, nz):
        pzcopy(k).wait_recv()
        wide = wide + pzbuf[k - 1]
    log_ref[...] = wide

    for s in range(nz):
        for j in range(1, nx):
            xcopy(s, j).wait_send()
            hcopy(s, j).wait_send()
    for k in range(1, nz):
        zcopy(k - 1).wait_send()
        gcopy(k).wait_send()
        pzcopy(k).wait_send()
    for j in range(1, nx):
        pxcopy(j).wait_send()


def series(n, nt, n_probes, w_in, w_out, start, mix, slope, u_slice):
    nx = max(2, nt // 4)
    nz = nt // nx
    depth, hidden = w_in[0].shape
    latents = depth * n
    chunk = latents // nt
    big = start.shape[0]
    rows = big // n_probes
    vmem = pl.BlockSpec(memory_space=pltpu.VMEM)
    bf, f32 = jnp.bfloat16, jnp.float32
    dma = pltpu.SemaphoreType.DMA
    return pl.pallas_call(
        functools.partial(series_kernel, n, nt, nx, n_probes),
        out_shape=(jax.ShapeDtypeStruct((rows, chunk), f32), jax.ShapeDtypeStruct((rows, 128), f32)),
        in_specs=[pl.BlockSpec(memory_space=pl.ANY)] * (2 * n) + [vmem] * 4,
        out_specs=(vmem, vmem),
        scratch_shapes=[
            pltpu.VMEM((latents, hidden), bf),
            pltpu.VMEM((latents, hidden), bf),
            pltpu.VMEM((big, hidden), bf),
            pltpu.VMEM((nt, 2 * big, chunk), bf),
            pltpu.VMEM((nz, nx - 1, 2 * big + rows, chunk), bf),
            pltpu.VMEM((nz, nx - 1, 2 * big + rows, chunk), bf),
            pltpu.VMEM((nz, 2 * big + rows, chunk), bf),
            pltpu.VMEM((nz - 1, 2 * big + rows, chunk), bf),
            pltpu.VMEM((big, hidden), f32),
            pltpu.VMEM((big, hidden), f32),
            pltpu.VMEM((2, rows, 128), f32),
            pltpu.VMEM((nx - 1, rows, 128), f32),
            pltpu.VMEM((nz - 1, rows, 128), f32),
            dma((n,)), dma((n,)),
            dma((nz, nx - 1)), dma((nz, nx - 1)),
            dma((nz - 1,)), dma((nz - 1,)),
            dma((nz - 1,)), dma((nz - 1,)),
            dma((nz, nx - 1)), dma((nz, nx - 1)),
            dma((nx - 1,)), dma((nx - 1,)),
            dma((nz - 1,)), dma((nz - 1,)),
        ],
        compiler_params=pltpu.CompilerParams(
            collective_id=0, has_side_effects=True, vmem_limit_bytes=61 * 1024 * 1024
        ),
        cost_estimate=pl.CostEstimate(
            flops=2 * big * latents * hidden * 6, bytes_accessed=4 * latents * hidden, transcendentals=0
        ),
    )(*w_in, *w_out, start, mix, slope, u_slice)


def make_local(n, t):
    def local(features, enc_in, enc_out, noise, in_weight, out_weight, probes):
        rows = features.shape[0]
        depth = in_weight.shape[0]
        latents = depth * n
        n_probes = probes.shape[0]
        w_in = gather_blocks(in_weight, n)
        w_out = gather_blocks(out_weight, n)
        own = owners(n)

        def cols(x):
            return [lax.dynamic_slice_in_dim(x, o * depth, depth, 1) for o in own]

        hidden = jax.nn.silu(dot(features, enc_in)).astype(jnp.bfloat16)
        partial_stats = dot(hidden, enc_out)
        moments = lax.psum_scatter(
            partial_stats.reshape(rows, 2, latents), "tensor", scatter_dimension=2, tiled=True
        )
        u_slice = (
            moments[:, 0] + jax.nn.softplus(moments[:, 1]) * noise.astype(jnp.float32)
        ).astype(jnp.bfloat16)
        u_full = lax.all_gather(u_slice, "tensor", axis=1, tiled=True)

        start = cols(probes.reshape(n_probes * rows, latents))
        q = sum(dot(a, w) for a, w in zip(start, w_in))
        pre_act = sum(dot(a, w) for a, w in zip(cols(u_full), w_in))
        tanh_val = jnp.tanh(pre_act)
        squash = tanh_val.astype(jnp.bfloat16)
        slope = 1.0 - tanh_val * tanh_val
        scaled = [
            (q[p * rows : (p + 1) * rows] * slope).astype(jnp.bfloat16) for p in range(n_probes)
        ]
        flowed, logdet = series(
            n, t, n_probes, w_in, w_out, probes.reshape(n_probes * rows, latents),
            jnp.concatenate(scaled + [squash], 0), slope, u_slice,
        )
        return flowed, logdet[:, 0]

    return local


def solution(mesh):
    in_specs = (
        P("dp", None),
        P(None, "tensor"),
        P("tensor", None),
        P("dp", "tensor"),
        P("dp", "tensor"),
        P("dp", "tensor"),
        P(None, "dp", None),
    )
    out_specs = (P("dp", "tensor"), P("dp"))
    local = make_local(mesh.shape["dp"], mesh.shape["tensor"])
    return jax.shard_map(local, mesh=mesh, in_specs=in_specs, out_specs=out_specs, check_vma=False)
```

```python
import functools

import jax
import jax.numpy as jnp
from jax import lax
from jax.experimental import pallas as pl
from jax.experimental.pallas import tpu as pltpu
from jax.sharding import PartitionSpec as P


def dot(a, b):
    return jnp.dot(a, b, preferred_element_type=jnp.float32)


def dot_t(a, b):
    return lax.dot_general(a, b, (((1,), (1,)), ((), ())), preferred_element_type=jnp.float32)


def gather_blocks(shard, n):
    half = n // 2
    swap = [(d, d ^ 1) for d in range(n)]
    blocks = []
    for k in range(half):
        own = shard
        if k:
            own = lax.ppermute(
                shard, "dp", [(((y + k) % half) * 2 + c, y * 2 + c) for y in range(half) for c in range(2)]
            )
        blocks += [own, lax.ppermute(own, "dp", swap)]
    return blocks


def owners(n):
    me = lax.axis_index("dp")
    core = lax.rem(me, 2)
    y = lax.div(me, 2)
    half = n // 2
    out = []
    for k in range(half):
        yk = lax.rem(y + k, half)
        out += [yk * 2 + core, yk * 2 + 1 - core]
    return out


def series_kernel(n, nt, nx, n_probes, *refs):
    w_in = refs[:n]
    w_shard, lhs, u_ref, flowed_ref, log_ref = refs[n : n + 5]
    (win, wout, sr, mix, slope, full, sendx, xbuf, own, zbuf, left, right, pbuf, pxbuf, pzbuf,
     in_sem, out_sem, ys, yr, fs, fr, cs, cr,
     xs, xr, zs, zr, gs, gr, hs, hr, pxs, pxr, pzs, pzr) = refs[n + 5 :]
    nz = nt // nx
    half = n // 2
    depth, hidden = w_in[0].shape
    big, rows = sr.shape[0], slope.shape[0]
    chunk = win.shape[0] // nt
    pieces = depth // chunk
    tile = min(512, hidden)
    tiles = hidden // tile
    t = lax.axis_index("tensor")
    z, x = lax.div(t, nx), lax.rem(t, nx)
    me = lax.axis_index("dp")
    y, core = lax.div(me, 2), lax.rem(me, 2)
    mate = {"dp": y * 2 + 1 - core}
    held = owners(n)
    mesh_ids = pl.DeviceIdType.MESH
    W, M = 0, 1
    bands = (pl.ds(0, big), pl.ds(big, big + rows))
    gbands = (pl.ds(0, big), pl.ds(big, big))

    def dev(zz, xx):
        return {"tensor": zz * nx + xx}

    def zup(k):
        return lax.rem(z + k, nz)

    def xup(j):
        return lax.rem(x + j, nx)

    def remote(src, dst, ss, rs, to):
        return pltpu.make_async_remote_copy(
            src_ref=src, dst_ref=dst, send_sem=ss, recv_sem=rs, device_id=to, device_id_type=mesh_ids
        )

    def at(i):
        return pl.ds(pl.multiple_of(i * tile, tile), tile)

    def block(o):
        return pl.ds(pl.multiple_of(o * depth, depth), depth)

    def piece(o, p):
        return pl.ds(pl.multiple_of(o * depth + p * chunk, chunk), chunk)

    barrier = pltpu.get_barrier_semaphore()
    peers = [dev(z, xup(j)) for j in range(1, nx)] + [dev(zup(k), x) for k in range(1, nz)]
    peers += [{"dp": lax.rem(y + k, half) * 2 + core} for k in range(1, half)] + [mate]
    for peer in peers:
        pl.semaphore_signal(barrier, inc=1, device_id=peer, device_id_type=mesh_ids)
    pl.semaphore_wait(barrier, len(peers))

    def ycopy(k, p):
        return remote(
            w_shard.at[pl.ds(p * chunk, chunk)], wout.at[piece(me, p)], ys.at[k - 1, p], yr.at[k - 1, p],
            {"dp": lax.rem(y + half - k, half) * 2 + core},
        )

    def yarrive(k, p):
        part = wout.at[piece(held[2 * k], p)]
        return remote(part, part, ys.at[k - 1, p], yr.at[k - 1, p], mate)

    def fcopy(k, p, own_side=True):
        part = wout.at[piece(held[2 * k + (0 if own_side else 1)], p)]
        return remote(part, part, fs.at[k - 1, p], fr.at[k - 1, p], mate)

    def ccopy(o):
        return remote(w_shard, wout.at[block(o)], cs, cr, mate)

    for k in range(1, half):
        ycopy(k, 0).start()
    loads_in = [pltpu.make_async_copy(w_in[b], win.at[block(held[b])], in_sem.at[b]) for b in range(n)]
    for c in loads_in:
        c.start()
    load_out = pltpu.make_async_copy(w_shard, wout.at[block(me)], out_sem)
    load_out.start()
    ccopy(me).start()

    for b in range(n):
        loads_in[b].wait()

        def first_pass(i, _):
            value = dot(lhs[:, block(held[b])], win[block(held[b]), at(i)])
            left[:, at(i)] = value[:big] if b == 0 else left[:, at(i)] + value[:big]
            slope[:, at(i)] = value[big:] if b == 0 else slope[:, at(i)] + value[big:]
            return 0

        lax.fori_loop(0, tiles, first_pass, 0)
        if b == n // 2:
            for k in range(1, half):
                for p in range(1, pieces):
                    ycopy(k, p).start()

    def activate(i, _):
        th = jnp.tanh(slope[:, at(i)])
        mix[pl.ds(big, rows), at(i)] = th.astype(jnp.bfloat16)
        s = 1.0 - th * th
        slope[:, at(i)] = s
        for p in range(n_probes):
            band = pl.ds(p * rows, rows)
            mix[band, at(i)] = (left[band, at(i)] * s).astype(jnp.bfloat16)
        return 0

    lax.fori_loop(0, tiles, activate, 0)
    left[...] = jnp.zeros_like(left)
    right[...] = jnp.zeros_like(right)

    def xcopy(kind, zt, j):
        band = bands[kind]
        return remote(
            sendx.at[zt, j - 1, band], xbuf.at[zt, j - 1, band],
            xs.at[kind, zt, j - 1], xr.at[kind, zt, j - 1], dev(z, xup(j)),
        )

    def zcopy(kind, k):
        band = bands[kind]
        return remote(
            own.at[zup(k), band], zbuf.at[k - 1, band], zs.at[kind, k - 1], zr.at[kind, k - 1], dev(zup(k), x)
        )

    def finish(kind, zt):
        for j in range(1, nx):
            xcopy(kind, zt, j).wait_recv()
        for i in range(bands[kind].size // rows):
            band = pl.ds(bands[kind].start + i * rows, rows)
            value = own[zt, band, :].astype(jnp.float32)
            for j in range(1, nx):
                value += xbuf[zt, j - 1, band, :].astype(jnp.float32)
            own[zt, band, :] = value.astype(jnp.bfloat16)

        @pl.when(zt != z)
        def _():
            zcopy(kind, lax.rem(zt - z + nz, nz)).start()

    def summed(kind):
        for k in range(1, nz):
            zcopy(kind, k).wait_recv()
        for i in range(bands[kind].size // rows):
            band = pl.ds(bands[kind].start + i * rows, rows)
            value = own[z, band, :].astype(jnp.float32)
            for k in range(1, nz):
                value += zbuf[k - 1, band, :].astype(jnp.float32)
            if kind == M and i == n_probes:
                flowed_ref[...] = u_ref[...].astype(jnp.float32) + value
            else:
                full[t, band, :] = value.astype(jnp.bfloat16)

    def process(o, p):
        off = piece(o, p)

        def pull(i, _):
            right[:, at(i)] += dot(lhs[pl.ds(0, big), off], wout[off, at(i)])
            return 0

        lax.fori_loop(0, tiles, pull, 0)
        target = o * pieces + p
        zt, xt = lax.div(target, nx), lax.rem(target, nx)
        jj = lax.rem(xt - x + nx, nx)
        value = dot_t(mix[...], wout[off, :]).astype(jnp.bfloat16)

        @pl.when(jj == 0)
        def _():
            own[zt, bands[M], :] = value

        @pl.when(jj != 0)
        def _():
            sendx[zt, jj - 1, bands[M], :] = value
            xcopy(M, zt, jj).start()

    def whole_block(o):
        def body(p, _):
            process(o, p)
            return 0

        lax.fori_loop(0, pieces, body, 0)

    def group_rows(k):
        a, b = held[2 * k], held[2 * k + 1]
        return [a, b] if n == nz else [lax.div(a, n // nz)]

    load_out.wait()
    whole_block(me)
    ccopy(held[1]).wait_recv()
    whole_block(held[1])
    for k in range(1, half):
        for p in range(pieces):
            yarrive(k, p).wait_recv()
            fcopy(k, p).start()
            if p == 0:
                for zt in group_rows(k - 1):
                    finish(M, zt)
            process(held[2 * k], p)
            fcopy(k, p, False).wait_recv()
            process(held[2 * k + 1], p)

    totals = []
    for p in range(n_probes):
        band = pl.ds(p * rows, rows)

        def scale(i, acc):
            r = right[band, at(i)]
            sr[band, at(i)] = (r * slope[:, at(i)]).astype(jnp.bfloat16)
            return acc + jnp.sum(mix[band, at(i)].astype(jnp.float32) * r, axis=1, keepdims=True)

        totals.append(lax.fori_loop(0, tiles, scale, jnp.zeros((rows, 1), jnp.float32)))
    right[...] = jnp.zeros_like(right)

    def scatter(s, _):
        zt = zup(1 + s)
        for j in list(range(1, nx)) + [0]:
            off = pl.ds(pl.multiple_of((zt * nx + xup(j)) * chunk, chunk), chunk)
            value = dot_t(sr[...], win[off, :]).astype(jnp.bfloat16)
            if j:
                sendx[zt, j - 1, bands[W], :] = value
                xcopy(W, zt, j).start()
            else:
                own[zt, bands[W], :] = value

        @pl.when(s == 0)
        def _():
            for zz in group_rows(half - 1):
                finish(M, zz)

        @pl.when(s >= 1)
        def _():
            finish(W, zup(s))

        return 0

    lax.fori_loop(0, nz, scatter, 0)

    def gcopy(kind, k):
        part = full.at[t, gbands[kind]]
        return remote(part, part, gs.at[kind, k - 1], gr.at[kind, k - 1], dev(zup(k), x))

    def slot(k, j):
        return lax.rem(z + nz - k, nz) * nx + lax.rem(x + nx - j, nx)

    def garrive(kind, k):
        part = full.at[slot(k, 0), gbands[kind]]
        return remote(part, part, gs.at[kind, k - 1], gr.at[kind, k - 1], dev(zup(k), x))

    def hcopy(kind, k, j):
        part = full.at[slot(k, 0), gbands[kind]]
        return remote(part, part, hs.at[kind, k, j - 1], hr.at[kind, k, j - 1], dev(z, xup(j)))

    def harrive(kind, k, j):
        part = full.at[slot(k, j), gbands[kind]]
        return remote(part, part, hs.at[kind, k, j - 1], hr.at[kind, k, j - 1], dev(z, xup(j)))

    def consume(kind, c):
        off = pl.ds(pl.multiple_of(c * chunk, chunk), chunk)
        acc, weight = (left, win) if kind == M else (right, wout)

        def body(i, _):
            acc[:, at(i)] += dot(full[c, gbands[kind], :], weight[off, at(i)])
            return 0

        lax.fori_loop(0, tiles, body, 0)

    def send_own(kind):
        for k in range(1, nz):
            gcopy(kind, k).start()
        for j in range(1, nx):
            hcopy(kind, 0, j).start()

    summed(M)
    send_own(M)
    finish(W, z)
    consume(M, t)
    summed(W)
    send_own(W)
    for p in range(n_probes):
        w1 = full[t, pl.ds(p * rows, rows), :].astype(jnp.float32)
        y1 = full[t, pl.ds(big + p * rows, rows), :].astype(jnp.float32)
        totals[p] -= 0.5 * jnp.sum(w1 * y1, axis=1, keepdims=True)
    consume(W, t)

    def gather(k, _):
        for kind in (M, W):
            garrive(kind, k).wait_recv()
            for j in range(1, nx):
                hcopy(kind, k, j).start()
            consume(kind, slot(k, 0))
        for kind in (M, W):
            for j in range(1, nx):
                harrive(kind, k - 1, j).wait_recv()
                consume(kind, slot(k - 1, j))
        return 0

    lax.fori_loop(1, nz, gather, 0)
    for kind in (M, W):
        for j in range(1, nx):
            harrive(kind, nz - 1, j).wait_recv()
            consume(kind, slot(nz - 1, j))

    total = jnp.zeros((rows, 1), jnp.float32)
    for p in range(n_probes):
        band = pl.ds(p * rows, rows)

        def last(i, acc):
            return acc + jnp.sum(left[band, at(i)] * slope[:, at(i)] * right[band, at(i)], axis=1, keepdims=True)

        third = lax.fori_loop(0, tiles, last, jnp.zeros((rows, 1), jnp.float32))
        total += totals[p] + third / 3.0

    def pxcopy(j):
        return remote(pbuf.at[0], pxbuf.at[j - 1], pxs.at[j - 1], pxr.at[j - 1], dev(z, xup(j)))

    def pzcopy(k):
        return remote(pbuf.at[1], pzbuf.at[k - 1], pzs.at[k - 1], pzr.at[k - 1], dev(zup(k), x))

    wide = jnp.broadcast_to(total / n_probes, (rows, 128))
    pbuf[0] = wide
    for j in range(1, nx):
        pxcopy(j).start()
    for j in range(1, nx):
        pxcopy(j).wait_recv()
        wide = wide + pxbuf[j - 1]
    pbuf[1] = wide
    for k in range(1, nz):
        pzcopy(k).start()
    for k in range(1, nz):
        pzcopy(k).wait_recv()
        wide = wide + pzbuf[k - 1]
    log_ref[...] = wide

    for kind in (W, M):
        for s in range(nz):
            for j in range(1, nx):
                xcopy(kind, s, j).wait_send()
                hcopy(kind, s, j).wait_send()
        for k in range(1, nz):
            zcopy(kind, k).wait_send()
            gcopy(kind, k).wait_send()
    for k in range(1, nz):
        pzcopy(k).wait_send()
    for j in range(1, nx):
        pxcopy(j).wait_send()
    ccopy(me).wait_send()
    for k in range(1, half):
        for p in range(pieces):
            ycopy(k, p).wait_send()
            fcopy(k, p).wait_send()


def series(n, nt, n_probes, w_in, w_shard, lhs, u_slice):
    nx = max(2, nt // 4)
    nz = nt // nx
    depth, hidden = w_in[0].shape
    latents = depth * n
    chunk = latents // nt
    pieces = depth // chunk
    rows = u_slice.shape[0]
    big = n_probes * rows
    half = n // 2
    vmem = pl.BlockSpec(memory_space=pltpu.VMEM)
    bf, f32 = jnp.bfloat16, jnp.float32
    dma = pltpu.SemaphoreType.DMA
    return pl.pallas_call(
        functools.partial(series_kernel, n, nt, nx, n_probes),
        out_shape=(jax.ShapeDtypeStruct((rows, chunk), f32), jax.ShapeDtypeStruct((rows, 128), f32)),
        in_specs=[pl.BlockSpec(memory_space=pl.ANY)] * (n + 1) + [vmem] * 2,
        out_specs=(vmem, vmem),
        scratch_shapes=[
            pltpu.VMEM((latents, hidden), bf),
            pltpu.VMEM((latents, hidden), bf),
            pltpu.VMEM((big, hidden), bf),
            pltpu.VMEM((big + rows, hidden), bf),
            pltpu.VMEM((rows, hidden), f32),
            pltpu.VMEM((nt, 2 * big, chunk), bf),
            pltpu.VMEM((nz, nx - 1, 2 * big + rows, chunk), bf),
            pltpu.VMEM((nz, nx - 1, 2 * big + rows, chunk), bf),
            pltpu.VMEM((nz, 2 * big + rows, chunk), bf),
            pltpu.VMEM((nz - 1, 2 * big + rows, chunk), bf),
            pltpu.VMEM((big, hidden), f32),
            pltpu.VMEM((big, hidden), f32),
            pltpu.VMEM((2, rows, 128), f32),
            pltpu.VMEM((nx - 1, rows, 128), f32),
            pltpu.VMEM((nz - 1, rows, 128), f32),
            dma((n,)), dma,
            dma((half - 1, pieces)), dma((half - 1, pieces)),
            dma((half - 1, pieces)), dma((half - 1, pieces)),
            dma, dma,
            dma((2, nz, nx - 1)), dma((2, nz, nx - 1)),
            dma((2, nz - 1)), dma((2, nz - 1)),
            dma((2, nz - 1)), dma((2, nz - 1)),
            dma((2, nz, nx - 1)), dma((2, nz, nx - 1)),
            dma((nx - 1,)), dma((nx - 1,)),
            dma((nz - 1,)), dma((nz - 1,)),
        ],
        compiler_params=pltpu.CompilerParams(
            collective_id=0, has_side_effects=True, vmem_limit_bytes=62 * 1024 * 1024
        ),
        cost_estimate=pl.CostEstimate(
            flops=2 * big * latents * hidden * 6, bytes_accessed=4 * latents * hidden, transcendentals=0
        ),
    )(*w_in, w_shard, lhs, u_slice)


def make_local(n, t):
    def local(features, enc_in, enc_out, noise, in_weight, out_weight, probes):
        rows = features.shape[0]
        depth = in_weight.shape[0]
        latents = depth * n
        n_probes = probes.shape[0]
        w_in = gather_blocks(in_weight, n)
        hidden = jax.nn.silu(dot(features, enc_in)).astype(jnp.bfloat16)
        partial_stats = dot(hidden, enc_out)
        moments = lax.psum_scatter(
            partial_stats.astype(jnp.bfloat16).reshape(rows, 2, latents), "tensor", scatter_dimension=2, tiled=True
        )
        moments = moments.astype(jnp.float32)
        u_slice = (
            moments[:, 0] + jax.nn.softplus(moments[:, 1]) * noise.astype(jnp.float32)
        ).astype(jnp.bfloat16)
        u_full = lax.all_gather(u_slice, "tensor", axis=1, tiled=True)

        lhs = jnp.concatenate([probes.reshape(n_probes * rows, latents), u_full], 0)
        flowed, logdet = series(n, t, n_probes, w_in, out_weight, lhs, u_slice)
        return flowed, logdet[:, 0]

    return local


def solution(mesh):
    in_specs = (
        P("dp", None),
        P(None, "tensor"),
        P("tensor", None),
        P("dp", "tensor"),
        P("dp", "tensor"),
        P("dp", "tensor"),
        P(None, "dp", None),
    )
    out_specs = (P("dp", "tensor"), P("dp"))
    local = make_local(mesh.shape["dp"], mesh.shape["tensor"])
    return jax.shard_map(local, mesh=mesh, in_specs=in_specs, out_specs=out_specs, check_vma=False)
```

```python
import functools

import jax
import jax.numpy as jnp
from jax import lax
from jax.experimental import pallas as pl
from jax.experimental.pallas import tpu as pltpu
from jax.sharding import PartitionSpec as P


def dot(a, b):
    return jnp.dot(a, b, preferred_element_type=jnp.float32)


def dot_t(a, b):
    return lax.dot_general(a, b, (((1,), (1,)), ((), ())), preferred_element_type=jnp.float32)


def gather_blocks(shard, n):
    half = n // 2
    swap = [(d, d ^ 1) for d in range(n)]
    blocks = []
    for k in range(half):
        own = shard
        if k:
            own = lax.ppermute(
                shard, "dp", [(((y + k) % half) * 2 + c, y * 2 + c) for y in range(half) for c in range(2)]
            )
        blocks += [own, lax.ppermute(own, "dp", swap)]
    return blocks


def owners(n):
    me = lax.axis_index("dp")
    core = lax.rem(me, 2)
    y = lax.div(me, 2)
    half = n // 2
    out = []
    for k in range(half):
        yk = lax.rem(y + k, half)
        out += [yk * 2 + core, yk * 2 + 1 - core]
    return out


def series_kernel(n, nt, nx, n_probes, *refs):
    w_in = refs[:n]
    w_shard, lhs, u_ref, flowed_ref, log_ref = refs[n : n + 5]
    (win, wout, sr, mix, slope, full, sendx, xbuf, own, zbuf, left, right, pbuf, pxbuf, pzbuf,
     ubuf, in_sem, out_sem, ys, yr, fs, fr, cs, cr, us, ur, vs, vr,
     xs, xr, zs, zr, gs, gr, hs, hr, pxs, pxr, pzs, pzr) = refs[n + 5 :]
    nz = nt // nx
    half = n // 2
    depth, hidden = w_in[0].shape
    big, rows = sr.shape[0], slope.shape[0]
    chunk = win.shape[0] // nt
    pieces = depth // chunk
    tile = min(512, hidden)
    tiles = hidden // tile
    t = lax.axis_index("tensor")
    z, x = lax.div(t, nx), lax.rem(t, nx)
    me = lax.axis_index("dp")
    y, core = lax.div(me, 2), lax.rem(me, 2)
    mate = {"dp": y * 2 + 1 - core}
    held = owners(n)
    mesh_ids = pl.DeviceIdType.MESH
    W, M = 0, 1
    bands = (pl.ds(0, big), pl.ds(big, big + rows))
    gbands = (pl.ds(0, big), pl.ds(big, big))

    def dev(zz, xx):
        return {"tensor": zz * nx + xx}

    def zup(k):
        return lax.rem(z + k, nz)

    def xup(j):
        return lax.rem(x + j, nx)

    def remote(src, dst, ss, rs, to):
        return pltpu.make_async_remote_copy(
            src_ref=src, dst_ref=dst, send_sem=ss, recv_sem=rs, device_id=to, device_id_type=mesh_ids
        )

    def at(i):
        return pl.ds(pl.multiple_of(i * tile, tile), tile)

    def block(o):
        return pl.ds(pl.multiple_of(o * depth, depth), depth)

    def piece(o, p):
        return pl.ds(pl.multiple_of(o * depth + p * chunk, chunk), chunk)

    barrier = pltpu.get_barrier_semaphore()
    peers = [dev(z, xup(j)) for j in range(1, nx)] + [dev(zup(k), x) for k in range(1, nz)]
    peers += [{"dp": lax.rem(y + k, half) * 2 + core} for k in range(1, half)] + [mate]
    for peer in peers:
        pl.semaphore_signal(barrier, inc=1, device_id=peer, device_id_type=mesh_ids)
    pl.semaphore_wait(barrier, len(peers))

    def ycopy(k, p):
        return remote(
            w_shard.at[pl.ds(p * chunk, chunk)], wout.at[piece(me, p)], ys.at[k - 1, p], yr.at[k - 1, p],
            {"dp": lax.rem(y + half - k, half) * 2 + core},
        )

    def yarrive(k, p):
        part = wout.at[piece(held[2 * k], p)]
        return remote(part, part, ys.at[k - 1, p], yr.at[k - 1, p], mate)

    def fcopy(k, p, own_side=True):
        part = wout.at[piece(held[2 * k + (0 if own_side else 1)], p)]
        return remote(part, part, fs.at[k - 1, p], fr.at[k - 1, p], mate)

    def ccopy(o):
        return remote(w_shard, wout.at[block(o)], cs, cr, mate)

    for k in range(1, half):
        ycopy(k, 0).start()
    loads_in = [pltpu.make_async_copy(w_in[b], win.at[block(held[b])], in_sem.at[b]) for b in range(n)]
    for c in loads_in:
        c.start()
    load_out = pltpu.make_async_copy(w_shard, wout.at[block(me)], out_sem)
    load_out.start()
    ccopy(me).start()

    def slot(k, j):
        return lax.rem(z + nz - k, nz) * nx + lax.rem(x + nx - j, nx)

    def ucopy(k):
        return remote(ubuf.at[t], ubuf.at[t], us.at[k - 1], ur.at[k - 1], dev(zup(k), x))

    def uarrive(k):
        part = ubuf.at[slot(k, 0)]
        return remote(part, part, us.at[k - 1], ur.at[k - 1], dev(zup(k), x))

    def vcopy(k, j):
        part = ubuf.at[slot(k, 0)]
        return remote(part, part, vs.at[k, j - 1], vr.at[k, j - 1], dev(z, xup(j)))

    def varrive(k, j):
        part = ubuf.at[slot(k, j)]
        return remote(part, part, vs.at[k, j - 1], vr.at[k, j - 1], dev(z, xup(j)))

    ubuf[t] = u_ref[...]
    for k in range(1, nz):
        ucopy(k).start()
    for j in range(1, nx):
        vcopy(0, j).start()

    for c in loads_in:
        c.wait()

    def first_pass(i, _):
        left[:, at(i)] = dot(lhs[...], win[:, at(i)])
        return 0

    lax.fori_loop(0, tiles, first_pass, 0)
    for k in range(1, half):
        for p in range(1, pieces):
            ycopy(k, p).start()
    for k in range(1, nz):
        uarrive(k).wait_recv()
        for j in range(1, nx):
            vcopy(k, j).start()
    for k in range(nz):
        for j in range(1, nx):
            varrive(k, j).wait_recv()

    def second_pass(i, _):
        slope[:, at(i)] = sum(
            dot(ubuf[c], win[pl.ds(c * chunk, chunk), at(i)]) for c in range(nt)
        )
        return 0

    lax.fori_loop(0, tiles, second_pass, 0)

    def activate(i, _):
        th = jnp.tanh(slope[:, at(i)])
        mix[pl.ds(big, rows), at(i)] = th.astype(jnp.bfloat16)
        s = 1.0 - th * th
        slope[:, at(i)] = s
        for p in range(n_probes):
            band = pl.ds(p * rows, rows)
            mix[band, at(i)] = (left[band, at(i)] * s).astype(jnp.bfloat16)
        return 0

    lax.fori_loop(0, tiles, activate, 0)
    left[...] = jnp.zeros_like(left)
    right[...] = jnp.zeros_like(right)

    def xcopy(kind, zt, j):
        band = bands[kind]
        return remote(
            sendx.at[zt, j - 1, band], xbuf.at[zt, j - 1, band],
            xs.at[kind, zt, j - 1], xr.at[kind, zt, j - 1], dev(z, xup(j)),
        )

    def zcopy(kind, k):
        band = bands[kind]
        return remote(
            own.at[zup(k), band], zbuf.at[k - 1, band], zs.at[kind, k - 1], zr.at[kind, k - 1], dev(zup(k), x)
        )

    def finish(kind, zt):
        for j in range(1, nx):
            xcopy(kind, zt, j).wait_recv()
        for i in range(bands[kind].size // rows):
            band = pl.ds(bands[kind].start + i * rows, rows)
            value = own[zt, band, :].astype(jnp.float32)
            for j in range(1, nx):
                value += xbuf[zt, j - 1, band, :].astype(jnp.float32)
            own[zt, band, :] = value.astype(jnp.bfloat16)

        @pl.when(zt != z)
        def _():
            zcopy(kind, lax.rem(zt - z + nz, nz)).start()

    def summed(kind):
        for k in range(1, nz):
            zcopy(kind, k).wait_recv()
        for i in range(bands[kind].size // rows):
            band = pl.ds(bands[kind].start + i * rows, rows)
            value = own[z, band, :].astype(jnp.float32)
            for k in range(1, nz):
                value += zbuf[k - 1, band, :].astype(jnp.float32)
            if kind == M and i == n_probes:
                flowed_ref[...] = u_ref[...].astype(jnp.float32) + value
            else:
                full[t, band, :] = value.astype(jnp.bfloat16)

    def process(o, p):
        off = piece(o, p)

        def pull(i, _):
            right[:, at(i)] += dot(lhs[pl.ds(0, big), off], wout[off, at(i)])
            return 0

        lax.fori_loop(0, tiles, pull, 0)
        target = o * pieces + p
        zt, xt = lax.div(target, nx), lax.rem(target, nx)
        jj = lax.rem(xt - x + nx, nx)
        value = dot_t(mix[...], wout[off, :]).astype(jnp.bfloat16)

        @pl.when(jj == 0)
        def _():
            own[zt, bands[M], :] = value

        @pl.when(jj != 0)
        def _():
            sendx[zt, jj - 1, bands[M], :] = value
            xcopy(M, zt, jj).start()

    def whole_block(o):
        def body(p, _):
            process(o, p)
            return 0

        lax.fori_loop(0, pieces, body, 0)

    def group_rows(k):
        a, b = held[2 * k], held[2 * k + 1]
        return [a, b] if n == nz else [lax.div(a, n // nz)]

    def gcopy(kind, k):
        part = full.at[t, gbands[kind]]
        return remote(part, part, gs.at[kind, k - 1], gr.at[kind, k - 1], dev(zup(k), x))

    def garrive(kind, k):
        part = full.at[slot(k, 0), gbands[kind]]
        return remote(part, part, gs.at[kind, k - 1], gr.at[kind, k - 1], dev(zup(k), x))

    def hcopy(kind, k, j):
        part = full.at[slot(k, 0), gbands[kind]]
        return remote(part, part, hs.at[kind, k, j - 1], hr.at[kind, k, j - 1], dev(z, xup(j)))

    def harrive(kind, k, j):
        part = full.at[slot(k, j), gbands[kind]]
        return remote(part, part, hs.at[kind, k, j - 1], hr.at[kind, k, j - 1], dev(z, xup(j)))

    def send_own(kind):
        for k in range(1, nz):
            gcopy(kind, k).start()
        for j in range(1, nx):
            hcopy(kind, 0, j).start()

    early = jnp.bool_(False)
    if pieces > 1:
        for k in range(half - 1):
            for zt in group_rows(k):
                early = jnp.logical_or(early, z == zt)

    def finish_rows():
        summed(M)
        send_own(M)

    load_out.wait()
    whole_block(me)
    ccopy(held[1]).wait_recv()
    whole_block(held[1])
    for k in range(1, half):
        for p in range(pieces):
            if k == half - 1 and p and p == pieces - 1:
                pl.when(early)(finish_rows)
            yarrive(k, p).wait_recv()
            fcopy(k, p).start()
            if p == 0:
                for zt in group_rows(k - 1):
                    finish(M, zt)
            process(held[2 * k], p)
            fcopy(k, p, False).wait_recv()
            process(held[2 * k + 1], p)

    totals = []
    for p in range(n_probes):
        band = pl.ds(p * rows, rows)

        def scale(i, acc):
            r = right[band, at(i)]
            sr[band, at(i)] = (r * slope[:, at(i)]).astype(jnp.bfloat16)
            return acc + jnp.sum(mix[band, at(i)].astype(jnp.float32) * r, axis=1, keepdims=True)

        totals.append(lax.fori_loop(0, tiles, scale, jnp.zeros((rows, 1), jnp.float32)))
    right[...] = jnp.zeros_like(right)

    def scatter(s, _):
        zt = zup(1 + s)
        for j in list(range(1, nx)) + [0]:
            off = pl.ds(pl.multiple_of((zt * nx + xup(j)) * chunk, chunk), chunk)
            value = dot_t(sr[...], win[off, :]).astype(jnp.bfloat16)
            if j:
                sendx[zt, j - 1, bands[W], :] = value
                xcopy(W, zt, j).start()
            else:
                own[zt, bands[W], :] = value

        @pl.when(s == 0)
        def _():
            for zz in group_rows(half - 1):
                finish(M, zz)

        @pl.when(s >= 1)
        def _():
            finish(W, zup(s))

        return 0

    lax.fori_loop(0, nz, scatter, 0)

    def consume(kind, c):
        off = pl.ds(pl.multiple_of(c * chunk, chunk), chunk)
        acc, weight = (left, win) if kind == M else (right, wout)

        def body(i, _):
            acc[:, at(i)] += dot(full[c, gbands[kind], :], weight[off, at(i)])
            return 0

        lax.fori_loop(0, tiles, body, 0)

    pl.when(jnp.logical_not(early))(finish_rows)
    finish(W, z)
    consume(M, t)
    summed(W)
    send_own(W)
    for p in range(n_probes):
        w1 = full[t, pl.ds(p * rows, rows), :].astype(jnp.float32)
        y1 = full[t, pl.ds(big + p * rows, rows), :].astype(jnp.float32)
        totals[p] -= 0.5 * jnp.sum(w1 * y1, axis=1, keepdims=True)
    consume(W, t)

    def gather(k, _):
        for kind in (M, W):
            garrive(kind, k).wait_recv()
            for j in range(1, nx):
                hcopy(kind, k, j).start()
            consume(kind, slot(k, 0))
        for kind in (M, W):
            for j in range(1, nx):
                harrive(kind, k - 1, j).wait_recv()
                consume(kind, slot(k - 1, j))
        return 0

    lax.fori_loop(1, nz, gather, 0)
    for kind in (M, W):
        for j in range(1, nx):
            harrive(kind, nz - 1, j).wait_recv()
            consume(kind, slot(nz - 1, j))

    total = jnp.zeros((rows, 1), jnp.float32)
    for p in range(n_probes):
        band = pl.ds(p * rows, rows)

        def last(i, acc):
            return acc + jnp.sum(left[band, at(i)] * slope[:, at(i)] * right[band, at(i)], axis=1, keepdims=True)

        third = lax.fori_loop(0, tiles, last, jnp.zeros((rows, 1), jnp.float32))
        total += totals[p] + third / 3.0

    def pxcopy(j):
        return remote(pbuf.at[0], pxbuf.at[j - 1], pxs.at[j - 1], pxr.at[j - 1], dev(z, xup(j)))

    def pzcopy(k):
        return remote(pbuf.at[1], pzbuf.at[k - 1], pzs.at[k - 1], pzr.at[k - 1], dev(zup(k), x))

    wide = jnp.broadcast_to(total / n_probes, (rows, 128))
    pbuf[0] = wide
    for j in range(1, nx):
        pxcopy(j).start()
    for j in range(1, nx):
        pxcopy(j).wait_recv()
        wide = wide + pxbuf[j - 1]
    pbuf[1] = wide
    for k in range(1, nz):
        pzcopy(k).start()
    for k in range(1, nz):
        pzcopy(k).wait_recv()
        wide = wide + pzbuf[k - 1]
    log_ref[...] = wide

    for kind in (W, M):
        for s in range(nz):
            for j in range(1, nx):
                xcopy(kind, s, j).wait_send()
                hcopy(kind, s, j).wait_send()
        for k in range(1, nz):
            zcopy(kind, k).wait_send()
            gcopy(kind, k).wait_send()
    for k in range(1, nz):
        pzcopy(k).wait_send()
    for j in range(1, nx):
        pxcopy(j).wait_send()
    for k in range(nz):
        for j in range(1, nx):
            vcopy(k, j).wait_send()
    for k in range(1, nz):
        ucopy(k).wait_send()
    ccopy(me).wait_send()
    for k in range(1, half):
        for p in range(pieces):
            ycopy(k, p).wait_send()
            fcopy(k, p).wait_send()


def series(n, nt, n_probes, w_in, w_shard, lhs, u_slice):
    nx = max(2, nt // 4)
    nz = nt // nx
    depth, hidden = w_in[0].shape
    latents = depth * n
    chunk = latents // nt
    pieces = depth // chunk
    rows = u_slice.shape[0]
    big = n_probes * rows
    half = n // 2
    vmem = pl.BlockSpec(memory_space=pltpu.VMEM)
    bf, f32 = jnp.bfloat16, jnp.float32
    dma = pltpu.SemaphoreType.DMA
    return pl.pallas_call(
        functools.partial(series_kernel, n, nt, nx, n_probes),
        out_shape=(jax.ShapeDtypeStruct((rows, chunk), f32), jax.ShapeDtypeStruct((rows, 128), f32)),
        in_specs=[pl.BlockSpec(memory_space=pl.ANY)] * (n + 1) + [vmem] * 2,
        out_specs=(vmem, vmem),
        scratch_shapes=[
            pltpu.VMEM((latents, hidden), bf),
            pltpu.VMEM((latents, hidden), bf),
            pltpu.VMEM((big, hidden), bf),
            pltpu.VMEM((big + rows, hidden), bf),
            pltpu.VMEM((rows, hidden), f32),
            pltpu.VMEM((nt, 2 * big, chunk), bf),
            pltpu.VMEM((nz, nx - 1, 2 * big + rows, chunk), bf),
            pltpu.VMEM((nz, nx - 1, 2 * big + rows, chunk), bf),
            pltpu.VMEM((nz, 2 * big + rows, chunk), bf),
            pltpu.VMEM((nz - 1, 2 * big + rows, chunk), bf),
            pltpu.VMEM((big, hidden), f32),
            pltpu.VMEM((big, hidden), f32),
            pltpu.VMEM((2, rows, 128), f32),
            pltpu.VMEM((nx - 1, rows, 128), f32),
            pltpu.VMEM((nz - 1, rows, 128), f32),
            pltpu.VMEM((nt, rows, chunk), bf),
            dma((n,)), dma,
            dma((half - 1, pieces)), dma((half - 1, pieces)),
            dma((half - 1, pieces)), dma((half - 1, pieces)),
            dma, dma,
            dma((nz - 1,)), dma((nz - 1,)),
            dma((nz, nx - 1)), dma((nz, nx - 1)),
            dma((2, nz, nx - 1)), dma((2, nz, nx - 1)),
            dma((2, nz - 1)), dma((2, nz - 1)),
            dma((2, nz - 1)), dma((2, nz - 1)),
            dma((2, nz, nx - 1)), dma((2, nz, nx - 1)),
            dma((nx - 1,)), dma((nx - 1,)),
            dma((nz - 1,)), dma((nz - 1,)),
        ],
        compiler_params=pltpu.CompilerParams(
            collective_id=0, has_side_effects=True, vmem_limit_bytes=62 * 1024 * 1024
        ),
        cost_estimate=pl.CostEstimate(
            flops=2 * big * latents * hidden * 6, bytes_accessed=4 * latents * hidden, transcendentals=0
        ),
    )(*w_in, w_shard, lhs, u_slice)


def make_local(n, t):
    def local(features, enc_in, enc_out, noise, in_weight, out_weight, probes):
        rows = features.shape[0]
        depth = in_weight.shape[0]
        latents = depth * n
        n_probes = probes.shape[0]
        w_in = gather_blocks(in_weight, n)
        hidden = jax.nn.silu(dot(features, enc_in)).astype(jnp.bfloat16)
        partial_stats = dot(hidden, enc_out)
        moments = lax.psum_scatter(
            partial_stats.astype(jnp.bfloat16).reshape(rows, 2, latents), "tensor", scatter_dimension=2, tiled=True
        )
        moments = moments.astype(jnp.float32)
        u_slice = (
            moments[:, 0] + jax.nn.softplus(moments[:, 1]) * noise.astype(jnp.float32)
        ).astype(jnp.bfloat16)
        lhs = probes.reshape(n_probes * rows, latents)
        flowed, logdet = series(n, t, n_probes, w_in, out_weight, lhs, u_slice)
        return flowed, logdet[:, 0]

    return local


def solution(mesh):
    in_specs = (
        P("dp", None),
        P(None, "tensor"),
        P("tensor", None),
        P("dp", "tensor"),
        P("dp", "tensor"),
        P("dp", "tensor"),
        P(None, "dp", None),
    )
    out_specs = (P("dp", "tensor"), P("dp"))
    local = make_local(mesh.shape["dp"], mesh.shape["tensor"])
    return jax.shard_map(local, mesh=mesh, in_specs=in_specs, out_specs=out_specs, check_vma=False)
```

```python
import functools

import jax
import jax.numpy as jnp
from jax import lax
from jax.experimental import pallas as pl
from jax.experimental.pallas import tpu as pltpu
from jax.sharding import PartitionSpec as P


def dot(a, b):
    return jnp.dot(a, b, preferred_element_type=jnp.float32)


def dot_t(a, b):
    return lax.dot_general(a, b, (((1,), (1,)), ((), ())), preferred_element_type=jnp.float32)


def gather_blocks(shard, n):
    half = n // 2
    swap = [(d, d ^ 1) for d in range(n)]
    blocks = []
    for k in range(half):
        own = shard
        if k:
            own = lax.ppermute(
                shard, "dp", [(((y + k) % half) * 2 + c, y * 2 + c) for y in range(half) for c in range(2)]
            )
        blocks += [own, lax.ppermute(own, "dp", swap)]
    return blocks


def owners(n):
    me = lax.axis_index("dp")
    core = lax.rem(me, 2)
    y = lax.div(me, 2)
    half = n // 2
    out = []
    for k in range(half):
        yk = lax.rem(y + k, half)
        out += [yk * 2 + core, yk * 2 + 1 - core]
    return out


def series_kernel(n, nt, nx, n_probes, *refs):
    w_in = refs[:n]
    w_shard, lhs, u_ref, flowed_ref, log_ref = refs[n : n + 5]
    (win, wout, sr, mix, slope, full, sendx, xbuf, own, zbuf, left, right, pbuf, pxbuf, pzbuf,
     ubuf, in_sem, out_sem, ys, yr, fs, fr, cs, cr, us, ur, vs, vr,
     xs, xr, zs, zr, gs, gr, hs, hr, pxs, pxr, pzs, pzr) = refs[n + 5 :]
    nz = nt // nx
    half = n // 2
    depth, hidden = w_in[0].shape
    big, rows = sr.shape[0], slope.shape[0]
    chunk = win.shape[0] // nt
    pieces = depth // chunk
    tile = min(512, hidden)
    tiles = hidden // tile
    t = lax.axis_index("tensor")
    z, x = lax.div(t, nx), lax.rem(t, nx)
    me = lax.axis_index("dp")
    y, core = lax.div(me, 2), lax.rem(me, 2)
    mate = {"dp": y * 2 + 1 - core}
    held = owners(n)
    mesh_ids = pl.DeviceIdType.MESH
    W, M = 0, 1
    bands = (pl.ds(0, big), pl.ds(big, big + rows))
    gbands = (pl.ds(0, big), pl.ds(big, big))

    def dev(zz, xx):
        return {"tensor": zz * nx + xx}

    def zup(k):
        return lax.rem(z + k, nz)

    def xup(j):
        return lax.rem(x + j, nx)

    def remote(src, dst, ss, rs, to):
        return pltpu.make_async_remote_copy(
            src_ref=src, dst_ref=dst, send_sem=ss, recv_sem=rs, device_id=to, device_id_type=mesh_ids
        )

    def at(i):
        return pl.ds(pl.multiple_of(i * tile, tile), tile)

    def block(o):
        return pl.ds(pl.multiple_of(o * depth, depth), depth)

    def piece(o, p):
        return pl.ds(pl.multiple_of(o * depth + p * chunk, chunk), chunk)

    barrier = pltpu.get_barrier_semaphore()
    peers = [dev(z, xup(j)) for j in range(1, nx)] + [dev(zup(k), x) for k in range(1, nz)]
    peers += [{"dp": lax.rem(y + k, half) * 2 + core} for k in range(1, half)] + [mate]
    for peer in peers:
        pl.semaphore_signal(barrier, inc=1, device_id=peer, device_id_type=mesh_ids)
    pl.semaphore_wait(barrier, len(peers))

    def ycopy(k, p):
        return remote(
            w_shard.at[pl.ds(p * chunk, chunk)], wout.at[piece(me, p)], ys.at[k - 1, p], yr.at[k - 1, p],
            {"dp": lax.rem(y + half - k, half) * 2 + core},
        )

    def yarrive(k, p):
        part = wout.at[piece(held[2 * k], p)]
        return remote(part, part, ys.at[k - 1, p], yr.at[k - 1, p], mate)

    def fcopy(k, p, own_side=True):
        part = wout.at[piece(held[2 * k + (0 if own_side else 1)], p)]
        return remote(part, part, fs.at[k - 1, p], fr.at[k - 1, p], mate)

    def ccopy(o):
        return remote(w_shard, wout.at[block(o)], cs, cr, mate)

    for k in range(1, half):
        ycopy(k, 0).start()
    loads_in = [pltpu.make_async_copy(w_in[b], win.at[block(held[b])], in_sem.at[b]) for b in range(n)]
    for c in loads_in:
        c.start()
    load_out = pltpu.make_async_copy(w_shard, wout.at[block(me)], out_sem)
    load_out.start()
    ccopy(me).start()

    def slot(k, j):
        return lax.rem(z + nz - k, nz) * nx + lax.rem(x + nx - j, nx)

    def ucopy(k):
        return remote(ubuf.at[t], ubuf.at[t], us.at[k - 1], ur.at[k - 1], dev(zup(k), x))

    def uarrive(k):
        part = ubuf.at[slot(k, 0)]
        return remote(part, part, us.at[k - 1], ur.at[k - 1], dev(zup(k), x))

    def vcopy(k, j):
        part = ubuf.at[slot(k, 0)]
        return remote(part, part, vs.at[k, j - 1], vr.at[k, j - 1], dev(z, xup(j)))

    def varrive(k, j):
        part = ubuf.at[slot(k, j)]
        return remote(part, part, vs.at[k, j - 1], vr.at[k, j - 1], dev(z, xup(j)))

    ubuf[t] = u_ref[...]
    for k in range(1, nz):
        ucopy(k).start()
    for j in range(1, nx):
        vcopy(0, j).start()

    for c in loads_in:
        c.wait()

    def first_pass(i, _):
        left[:, at(i)] = dot(lhs[...], win[:, at(i)])
        return 0

    lax.fori_loop(0, tiles, first_pass, 0)
    for k in range(1, half):
        for p in range(1, pieces):
            ycopy(k, p).start()
    for k in range(1, nz):
        uarrive(k).wait_recv()
        for j in range(1, nx):
            vcopy(k, j).start()
    for k in range(nz):
        for j in range(1, nx):
            varrive(k, j).wait_recv()

    def second_pass(i, _):
        slope[:, at(i)] = sum(
            dot(ubuf[c], win[pl.ds(c * chunk, chunk), at(i)]) for c in range(nt)
        )
        return 0

    lax.fori_loop(0, tiles, second_pass, 0)

    def activate(i, _):
        th = jnp.tanh(slope[:, at(i)])
        mix[pl.ds(big, rows), at(i)] = th.astype(jnp.bfloat16)
        s = 1.0 - th * th
        slope[:, at(i)] = s
        for p in range(n_probes):
            band = pl.ds(p * rows, rows)
            mix[band, at(i)] = (left[band, at(i)] * s).astype(jnp.bfloat16)
        return 0

    lax.fori_loop(0, tiles, activate, 0)
    left[...] = jnp.zeros_like(left)
    right[...] = jnp.zeros_like(right)

    def xcopy(kind, zt, j):
        band = bands[kind]
        return remote(
            sendx.at[zt, j - 1, band], xbuf.at[zt, j - 1, band],
            xs.at[kind, zt, j - 1], xr.at[kind, zt, j - 1], dev(z, xup(j)),
        )

    def zcopy(kind, k):
        band = bands[kind]
        return remote(
            own.at[zup(k), band], zbuf.at[k - 1, band], zs.at[kind, k - 1], zr.at[kind, k - 1], dev(zup(k), x)
        )

    def finish(kind, zt):
        for j in range(1, nx):
            xcopy(kind, zt, j).wait_recv()
        for i in range(bands[kind].size // rows):
            band = pl.ds(bands[kind].start + i * rows, rows)
            value = own[zt, band, :].astype(jnp.float32)
            for j in range(1, nx):
                value += xbuf[zt, j - 1, band, :].astype(jnp.float32)
            own[zt, band, :] = value.astype(jnp.bfloat16)

        @pl.when(zt != z)
        def _():
            zcopy(kind, lax.rem(zt - z + nz, nz)).start()

    def summed(kind):
        for k in range(1, nz):
            zcopy(kind, k).wait_recv()
        for i in range(bands[kind].size // rows):
            band = pl.ds(bands[kind].start + i * rows, rows)
            value = own[z, band, :].astype(jnp.float32)
            for k in range(1, nz):
                value += zbuf[k - 1, band, :].astype(jnp.float32)
            if kind == M and i == n_probes:
                flowed_ref[...] = u_ref[...].astype(jnp.float32) + value
            else:
                full[t, band, :] = value.astype(jnp.bfloat16)

    def process(o, p):
        off = piece(o, p)

        def pull(i, _):
            right[:, at(i)] += dot(lhs[pl.ds(0, big), off], wout[off, at(i)])
            return 0

        lax.fori_loop(0, tiles, pull, 0)
        target = o * pieces + p
        zt, xt = lax.div(target, nx), lax.rem(target, nx)
        jj = lax.rem(xt - x + nx, nx)
        value = dot_t(mix[...], wout[off, :]).astype(jnp.bfloat16)

        @pl.when(jj == 0)
        def _():
            own[zt, bands[M], :] = value

        @pl.when(jj != 0)
        def _():
            sendx[zt, jj - 1, bands[M], :] = value
            xcopy(M, zt, jj).start()

    def whole_block(o):
        def body(p, _):
            process(o, p)
            return 0

        lax.fori_loop(0, pieces, body, 0)

    def group_rows(k):
        a, b = held[2 * k], held[2 * k + 1]
        return [a, b] if n == nz else [lax.div(a, n // nz)]

    def gcopy(kind, k):
        part = full.at[t, gbands[kind]]
        return remote(part, part, gs.at[kind, k - 1], gr.at[kind, k - 1], dev(zup(k), x))

    def garrive(kind, k):
        part = full.at[slot(k, 0), gbands[kind]]
        return remote(part, part, gs.at[kind, k - 1], gr.at[kind, k - 1], dev(zup(k), x))

    def hcopy(kind, k, j):
        part = full.at[slot(k, 0), gbands[kind]]
        return remote(part, part, hs.at[kind, k, j - 1], hr.at[kind, k, j - 1], dev(z, xup(j)))

    def harrive(kind, k, j):
        part = full.at[slot(k, j), gbands[kind]]
        return remote(part, part, hs.at[kind, k, j - 1], hr.at[kind, k, j - 1], dev(z, xup(j)))

    def send_own(kind):
        for k in range(1, nz):
            gcopy(kind, k).start()
        for j in range(1, nx):
            hcopy(kind, 0, j).start()

    def consume(kind, c):
        off = pl.ds(pl.multiple_of(c * chunk, chunk), chunk)
        acc, weight = (left, win) if kind == M else (right, wout)

        def body(i, _):
            acc[:, at(i)] += dot(full[c, gbands[kind], :], weight[off, at(i)])
            return 0

        lax.fori_loop(0, tiles, body, 0)

    def is_early(zz):
        found = jnp.bool_(False)
        for k in range(half - 1):
            for zt in group_rows(k):
                found = jnp.logical_or(found, zz == zt)
        return found

    def row(k):
        return lax.rem(z + nz - k, nz)

    early = is_early(z)

    def forward(kind, k):
        garrive(kind, k).wait_recv()
        for j in range(1, nx):
            hcopy(kind, k, j).start()
        consume(kind, slot(k, 0))

    def take(kind, k):
        for j in range(1, nx):
            harrive(kind, k, j).wait_recv()
            consume(kind, slot(k, j))

    def early_rows():
        pl.when(early)(lambda: consume(M, t))
        for k in range(1, nz):
            pl.when(is_early(row(k)))(functools.partial(forward, M, k))
        for k in range(nz):
            pl.when(is_early(row(k)))(functools.partial(take, M, k))

    def finish_rows():
        summed(M)
        send_own(M)

    load_out.wait()
    whole_block(me)
    ccopy(held[1]).wait_recv()
    whole_block(held[1])
    for k in range(1, half):
        for p in range(pieces):
            if p == 0:
                for zt in group_rows(k - 1):
                    finish(M, zt)
                if k == half - 1:
                    pl.when(early)(finish_rows)
            if k == half - 1 and p == pieces - 1:
                early_rows()
            yarrive(k, p).wait_recv()
            fcopy(k, p).start()
            process(held[2 * k], p)
            fcopy(k, p, False).wait_recv()
            process(held[2 * k + 1], p)

    totals = []
    for p in range(n_probes):
        band = pl.ds(p * rows, rows)

        def scale(i, acc):
            r = right[band, at(i)]
            sr[band, at(i)] = (r * slope[:, at(i)]).astype(jnp.bfloat16)
            return acc + jnp.sum(mix[band, at(i)].astype(jnp.float32) * r, axis=1, keepdims=True)

        totals.append(lax.fori_loop(0, tiles, scale, jnp.zeros((rows, 1), jnp.float32)))
    right[...] = jnp.zeros_like(right)

    def scatter(s, _):
        zt = zup(1 + s)
        for j in list(range(1, nx)) + [0]:
            off = pl.ds(pl.multiple_of((zt * nx + xup(j)) * chunk, chunk), chunk)
            value = dot_t(sr[...], win[off, :]).astype(jnp.bfloat16)
            if j:
                sendx[zt, j - 1, bands[W], :] = value
                xcopy(W, zt, j).start()
            else:
                own[zt, bands[W], :] = value

        @pl.when(s == 0)
        def _():
            for zz in group_rows(half - 1):
                finish(M, zz)

        @pl.when(s >= 1)
        def _():
            finish(W, zup(s))

        return 0

    lax.fori_loop(0, nz, scatter, 0)

    pl.when(jnp.logical_not(early))(finish_rows)
    finish(W, z)
    pl.when(jnp.logical_not(early))(lambda: consume(M, t))
    summed(W)
    send_own(W)
    for p in range(n_probes):
        w1 = full[t, pl.ds(p * rows, rows), :].astype(jnp.float32)
        y1 = full[t, pl.ds(big + p * rows, rows), :].astype(jnp.float32)
        totals[p] -= 0.5 * jnp.sum(w1 * y1, axis=1, keepdims=True)
    consume(W, t)

    def gather(k, _):
        pl.when(jnp.logical_not(is_early(row(k))))(lambda: forward(M, k))
        forward(W, k)
        pl.when(jnp.logical_not(is_early(row(k - 1))))(lambda: take(M, k - 1))
        take(W, k - 1)
        return 0

    lax.fori_loop(1, nz, gather, 0)
    pl.when(jnp.logical_not(is_early(row(nz - 1))))(lambda: take(M, nz - 1))
    take(W, nz - 1)

    total = jnp.zeros((rows, 1), jnp.float32)
    for p in range(n_probes):
        band = pl.ds(p * rows, rows)

        def last(i, acc):
            return acc + jnp.sum(left[band, at(i)] * slope[:, at(i)] * right[band, at(i)], axis=1, keepdims=True)

        third = lax.fori_loop(0, tiles, last, jnp.zeros((rows, 1), jnp.float32))
        total += totals[p] + third / 3.0

    def pxcopy(j):
        return remote(pbuf.at[0], pxbuf.at[j - 1], pxs.at[j - 1], pxr.at[j - 1], dev(z, xup(j)))

    def pzcopy(k):
        return remote(pbuf.at[1], pzbuf.at[k - 1], pzs.at[k - 1], pzr.at[k - 1], dev(zup(k), x))

    wide = jnp.broadcast_to(total / n_probes, (rows, 128))
    pbuf[0] = wide
    for j in range(1, nx):
        pxcopy(j).start()
    for j in range(1, nx):
        pxcopy(j).wait_recv()
        wide = wide + pxbuf[j - 1]
    pbuf[1] = wide
    for k in range(1, nz):
        pzcopy(k).start()
    for k in range(1, nz):
        pzcopy(k).wait_recv()
        wide = wide + pzbuf[k - 1]
    log_ref[...] = wide

    for kind in (W, M):
        for s in range(nz):
            for j in range(1, nx):
                xcopy(kind, s, j).wait_send()
                hcopy(kind, s, j).wait_send()
        for k in range(1, nz):
            zcopy(kind, k).wait_send()
            gcopy(kind, k).wait_send()
    for k in range(1, nz):
        pzcopy(k).wait_send()
    for j in range(1, nx):
        pxcopy(j).wait_send()
    for k in range(nz):
        for j in range(1, nx):
            vcopy(k, j).wait_send()
    for k in range(1, nz):
        ucopy(k).wait_send()
    ccopy(me).wait_send()
    for k in range(1, half):
        for p in range(pieces):
            ycopy(k, p).wait_send()
            fcopy(k, p).wait_send()


def series(n, nt, n_probes, w_in, w_shard, lhs, u_slice):
    nx = max(2, nt // 4)
    nz = nt // nx
    depth, hidden = w_in[0].shape
    latents = depth * n
    chunk = latents // nt
    pieces = depth // chunk
    rows = u_slice.shape[0]
    big = n_probes * rows
    half = n // 2
    vmem = pl.BlockSpec(memory_space=pltpu.VMEM)
    bf, f32 = jnp.bfloat16, jnp.float32
    dma = pltpu.SemaphoreType.DMA
    return pl.pallas_call(
        functools.partial(series_kernel, n, nt, nx, n_probes),
        out_shape=(jax.ShapeDtypeStruct((rows, chunk), f32), jax.ShapeDtypeStruct((rows, 128), f32)),
        in_specs=[pl.BlockSpec(memory_space=pl.ANY)] * (n + 1) + [vmem] * 2,
        out_specs=(vmem, vmem),
        scratch_shapes=[
            pltpu.VMEM((latents, hidden), bf),
            pltpu.VMEM((latents, hidden), bf),
            pltpu.VMEM((big, hidden), bf),
            pltpu.VMEM((big + rows, hidden), bf),
            pltpu.VMEM((rows, hidden), f32),
            pltpu.VMEM((nt, 2 * big, chunk), bf),
            pltpu.VMEM((nz, nx - 1, 2 * big + rows, chunk), bf),
            pltpu.VMEM((nz, nx - 1, 2 * big + rows, chunk), bf),
            pltpu.VMEM((nz, 2 * big + rows, chunk), bf),
            pltpu.VMEM((nz - 1, 2 * big + rows, chunk), bf),
            pltpu.VMEM((big, hidden), f32),
            pltpu.VMEM((big, hidden), f32),
            pltpu.VMEM((2, rows, 128), f32),
            pltpu.VMEM((nx - 1, rows, 128), f32),
            pltpu.VMEM((nz - 1, rows, 128), f32),
            pltpu.VMEM((nt, rows, chunk), bf),
            dma((n,)), dma,
            dma((half - 1, pieces)), dma((half - 1, pieces)),
            dma((half - 1, pieces)), dma((half - 1, pieces)),
            dma, dma,
            dma((nz - 1,)), dma((nz - 1,)),
            dma((nz, nx - 1)), dma((nz, nx - 1)),
            dma((2, nz, nx - 1)), dma((2, nz, nx - 1)),
            dma((2, nz - 1)), dma((2, nz - 1)),
            dma((2, nz - 1)), dma((2, nz - 1)),
            dma((2, nz, nx - 1)), dma((2, nz, nx - 1)),
            dma((nx - 1,)), dma((nx - 1,)),
            dma((nz - 1,)), dma((nz - 1,)),
        ],
        compiler_params=pltpu.CompilerParams(
            collective_id=0, has_side_effects=True, vmem_limit_bytes=62 * 1024 * 1024
        ),
        cost_estimate=pl.CostEstimate(
            flops=2 * big * latents * hidden * 6, bytes_accessed=4 * latents * hidden, transcendentals=0
        ),
    )(*w_in, w_shard, lhs, u_slice)


def make_local(n, t):
    def local(features, enc_in, enc_out, noise, in_weight, out_weight, probes):
        rows = features.shape[0]
        depth = in_weight.shape[0]
        latents = depth * n
        n_probes = probes.shape[0]
        w_in = gather_blocks(in_weight, n)
        hidden = jax.nn.silu(dot(features, enc_in)).astype(jnp.bfloat16)
        partial_stats = dot(hidden, enc_out)
        moments = lax.psum_scatter(
            partial_stats.astype(jnp.bfloat16).reshape(rows, 2, latents), "tensor", scatter_dimension=2, tiled=True
        )
        moments = moments.astype(jnp.float32)
        u_slice = (
            moments[:, 0] + jax.nn.softplus(moments[:, 1]) * noise.astype(jnp.float32)
        ).astype(jnp.bfloat16)
        lhs = probes.reshape(n_probes * rows, latents)
        flowed, logdet = series(n, t, n_probes, w_in, out_weight, lhs, u_slice)
        return flowed, logdet[:, 0]

    return local


def solution(mesh):
    in_specs = (
        P("dp", None),
        P(None, "tensor"),
        P("tensor", None),
        P("dp", "tensor"),
        P("dp", "tensor"),
        P("dp", "tensor"),
        P(None, "dp", None),
    )
    out_specs = (P("dp", "tensor"), P("dp"))
    local = make_local(mesh.shape["dp"], mesh.shape["tensor"])
    return jax.shard_map(local, mesh=mesh, in_specs=in_specs, out_specs=out_specs, check_vma=False)
```
